256 devices in a mesh: island: 16 (over y, z_hi), section: 8 (over z_lo, x), tp: 2 (over core).
Axes of the slice: x: 4, y: 4, z: 8 (z_hi: 4, z_lo: 2; z = z_hi * 2 + z_lo), core: 2. Of those that a mesh axis runs over, the one named last changes fastest.
Arguments:
- tokens: bfloat16 [3072, 3584], P('island', 'tp'), may hold values from -6 to 6
- cotangent: bfloat16 [3072, 3584], P('island', 'tp'), may hold values from -6 to 6
- master: float32 [8, 3584, 3584], P('section', 'island', 'tp'), may hold values from -0.09375 to 0.09375
Outputs:
- in_grads: bfloat16 [8, 3072, 3584], P('section', 'island', 'tp')
- new_master: float32 [8, 3584, 3584], P('section', 'island', 'tp')
The draws below stay inside these ranges and needn't reach their ends.
All inputs are finite; a program needn't handle non-finite values.
Results may differ from the reference program's by a relative error of at most 0.025.
Values may be sent and summed in bfloat16 or wider, within the bound.
No kernel may reach another device: no remote copies, remote signals or barrier semaphores. Data moves between devices by JAX's collectives and lax.ppermute only.
A program may use at most 64 MiB of HBM per device.

```python
import jax
import jax.numpy as jnp
from jax import lax

D = 3584
TOK = 192
TOKENS = 3072
SECTIONS = 8
N_ISLAND = 16
N_TP = 2


def with_spikes(result, key, source, target, blocks, factor):
    def block_of(axis_at):
        return (jnp.arange(result.shape[axis_at]) // (result.shape[axis_at] // blocks)).reshape((-1,) + (1,) * (result.ndim - 1 - axis_at))

    near = jax.random.permutation(key, blocks)[block_of(target)]
    second = (block_of(target) + blocks // 2) % blocks
    return jnp.where((block_of(source) == near) | (block_of(source) == second), factor * result, result)


def shard_levels(rng, shape, pieces, low, largest):
    def one(axis_at, blocks):
        steps = jax.random.uniform(jax.random.fold_in(jax.random.fold_in(rng, 6), axis_at), (blocks,), jnp.float32, low / len(pieces), largest / len(pieces))
        return jnp.repeat(jnp.exp(steps), shape[axis_at] // blocks).reshape((-1,) + (1,) * (len(shape) - axis_at - 1))

    gain = one(*pieces[0])
    for cut in pieces[1:]:
        gain = gain * one(*cut)
    return gain


def gaussian(key, shape, width, limit, split=(), held_as=jnp.bfloat16):
    result = width * jax.random.normal(key, shape, jnp.float32)
    if split:
        result = result * shard_levels(key, shape, split, -0.22, 0.18)
    return jnp.clip(result, -limit, limit).astype(held_as)


def bell_draw_with(own_key, dims, spread, most, cuts, heavy, dtype=jnp.bfloat16):
    drawn = spread * jax.random.normal(own_key, dims, jnp.float32)
    if cuts:
        drawn = drawn * shard_levels(own_key, dims, cuts, -0.22, 0.18)
    return jnp.clip(with_spikes(drawn, jax.random.fold_in(own_key, 3), *heavy), -most, most).astype(dtype)


def setup_inputs(seed: int = 0) -> dict:
    arg_keys = jax.random.split(jax.random.key(seed), 4)
    tokens = bell_draw_with(arg_keys[0], (TOKENS, D), 1.0, 6.0, ((0, 16), (1, 2)), (0, 1, 16, 2.0))
    cotangent = gaussian(arg_keys[1], (TOKENS, D), 1.0, 6.0, ((0, 16), (1, 2)))
    master = gaussian(arg_keys[2], (SECTIONS, D, D), D ** -0.5, 0.09375, ((0, 8), (1, 16), (2, 2)), jnp.float32)
    return dict(tokens=tokens, cotangent=cotangent, master=master)


NORM_EPS = 1e-05
STEP_SIZE = 1.0

def silu_slope(preact):
    sig_value = jax.nn.sigmoid(preact)
    return sig_value * (1.0 + preact * (1.0 - sig_value))

def reference(tokens, cotangent, master):
    weights = master.astype(jnp.bfloat16)
    half_width = D // N_TP
    x_now = tokens
    stash_list = []
    for section_at in range(SECTIONS):
        x_float = x_now.astype(jnp.float32)
        row_scale = lax.rsqrt(lax.optimization_barrier(jnp.mean(x_float * x_float, axis=1, keepdims=True)) + NORM_EPS)
        normed = (x_float * row_scale).astype(jnp.bfloat16)
        preact = jnp.dot(normed, weights[section_at], preferred_element_type=jnp.float32)
        stash_list.append((normed, preact, row_scale))
        x_now = (x_float + jax.nn.silu(preact)).astype(jnp.bfloat16)
    grad_now = cotangent
    in_grads = [None] * SECTIONS
    new_rows = [None] * SECTIONS
    for section_at in range(SECTIONS - 1, -1, -1):
        normed, preact, row_scale = stash_list[section_at]
        delta_now = (grad_now.astype(jnp.float32) * silu_slope(preact)).astype(jnp.bfloat16)
        summed = jnp.zeros((TOKENS, D), jnp.float32)
        for column_block in range(N_TP):
            lower_col = column_block * half_width
            partial_value = lax.dot_general(delta_now[:, lower_col:lower_col + half_width], weights[section_at][:, lower_col:lower_col + half_width], (((1,), (1,)), ((), ())), preferred_element_type=jnp.float32)
            rounded = lax.optimization_barrier(partial_value.astype(jnp.bfloat16))
            summed = summed + rounded.astype(jnp.float32)
        normed_float = normed.astype(jnp.float32)
        mean_prod = lax.optimization_barrier(jnp.sum(summed * normed_float, axis=1, keepdims=True)) / D
        grad_now = (grad_now.astype(jnp.float32) + row_scale * (summed - normed_float * mean_prod)).astype(jnp.bfloat16)
        in_grads[section_at] = grad_now

        def add_island(island_at, grad_total, normed=normed, delta_now=delta_now):
            row_start = (island_at * TOK).astype(jnp.int32)
            rows_norm = lax.dynamic_slice_in_dim(normed, row_start, TOK, 0)
            rows_delta = lax.dynamic_slice_in_dim(delta_now, row_start, TOK, 0)
            island_term = lax.dot_general(rows_norm, rows_delta, (((0,), (0,)), ((), ())), preferred_element_type=jnp.float32)
            rounded_term = lax.optimization_barrier(island_term.astype(jnp.bfloat16))
            return grad_total + rounded_term.astype(jnp.float32)
        grad_total = lax.fori_loop(0, N_ISLAND, add_island, jnp.zeros((D, D), jnp.float32))
        new_rows[section_at] = master[section_at] - STEP_SIZE * grad_total / TOKENS
    return (jnp.stack(in_grads), jnp.stack(new_rows))
```

```python
import jax
import jax.numpy as jnp
from jax import lax
from jax.experimental import pallas as pl
from jax.experimental.pallas import tpu as pltpu
from jax.sharding import PartitionSpec as P

D = 3584
HALF = 1792
MICRO = 4
MB = 48
SECTIONS = 8
TICKS = MICRO + SECTIONS - 1
NORM_EPS = 1e-05
STEP_SIZE = 1.0
F32 = jnp.float32
BF16 = jnp.bfloat16
N_TILE = 256
K_TILE = 256
PARAMS = pltpu.CompilerParams(vmem_limit_bytes=40 * 1024 * 1024)
VMEM = pl.BlockSpec(memory_space=pltpu.VMEM)
SMEM = pl.BlockSpec(memory_space=pltpu.SMEM)


def forward_kernel(ids, own, other, next_tokens, weights, send, preact, scale):
    tp_id = ids[0]
    is_last = ids[1] == SECTIONS - 1
    own_float = own[...].astype(F32)
    other_float = other[...].astype(F32)
    square_sum = jnp.sum(own_float * own_float, axis=1, keepdims=True)
    square_sum += jnp.sum(other_float * other_float, axis=1, keepdims=True)
    row_scale = lax.rsqrt(square_sum / D + NORM_EPS)
    scale[...] = jnp.broadcast_to(row_scale, scale.shape)
    for tile in range(HALF // N_TILE):
        cols = pl.ds(tile * N_TILE, N_TILE)
        product = jnp.dot(own[...], weights[tp_id, :, cols], preferred_element_type=F32)
        product += jnp.dot(other[...], weights[1 - tp_id, :, cols], preferred_element_type=F32)
        value = product * row_scale
        preact[:, cols] = value
        output = own[:, cols].astype(F32) + value / (1.0 + jnp.exp(-value))
        output = output.astype(BF16).astype(F32)
        send[:, cols] = jnp.where(is_last, next_tokens[:, cols].astype(F32), output).astype(BF16)


def forward_tick(ids, own, other, next_tokens, weights):
    return pl.pallas_call(
        forward_kernel,
        out_shape=(
            jax.ShapeDtypeStruct((MB, HALF), BF16),
            jax.ShapeDtypeStruct((MB, HALF), F32),
            jax.ShapeDtypeStruct((MB, 128), F32),
        ),
        in_specs=[SMEM, VMEM, VMEM, VMEM, VMEM],
        out_specs=(VMEM, VMEM, VMEM),
        compiler_params=PARAMS,
        name="forward_tick",
    )(ids, own, other, next_tokens, weights)


def backward_kernel(ids, grad, own, other, preact, scale, weights, scaled, own_part, other_part):
    tp_id = ids[0]
    row_scale = scale[:, :1]
    mean_prod = jnp.zeros((MB, 1), F32)
    for tile in range(HALF // N_TILE):
        cols = pl.ds(tile * N_TILE, N_TILE)
        value = preact[:, cols]
        sig_value = 1.0 / (1.0 + jnp.exp(-value))
        delta = grad[:, cols].astype(F32) * (sig_value * (1.0 + value * (1.0 - sig_value)))
        mean_prod += jnp.sum(delta * value, axis=1, keepdims=True)
        scaled[:, cols] = (delta * row_scale).astype(BF16)
    shift = row_scale * row_scale * (mean_prod / D)
    for tile in range(HALF // K_TILE):
        cols = pl.ds(tile * K_TILE, K_TILE)
        for half, x_ref, out in ((1 - tp_id, other, other_part), (tp_id, own, own_part)):
            product = lax.dot_general(
                scaled[...],
                weights[half, cols, :],
                (((1,), (1,)), ((), ())),
                preferred_element_type=F32,
            )
            product -= x_ref[:, cols].astype(F32) * shift
            out[:, cols] = product.astype(out.dtype)


def backward_tick(ids, grad, own, other, preact, scale, weights):
    return pl.pallas_call(
        backward_kernel,
        out_shape=(
            jax.ShapeDtypeStruct((MB, HALF), BF16),
            jax.ShapeDtypeStruct((MB, HALF), F32),
            jax.ShapeDtypeStruct((MB, HALF), BF16),
        ),
        in_specs=[SMEM] + [VMEM] * 6,
        out_specs=(VMEM, VMEM, VMEM),
        compiler_params=PARAMS,
        name="backward_tick",
    )(ids, grad, own, other, preact, scale, weights)


def swap_cores(value):
    return lax.ppermute(value, "tp", [(0, 1), (1, 0)])


def to_section(value, step):
    return lax.ppermute(value, "section", [(s, (s + step) % SECTIONS) for s in range(SECTIONS)])


def gather_weights(rows):
    return lax.all_gather(rows, "island", axis=0, tiled=True)


def scatter_grads(grads):
    return lax.psum_scatter(grads, "island", scatter_dimension=0, tiled=True)


def body(tokens, cotangent, master):
    island_count = lax.axis_size("island")
    section_id = lax.axis_index("section")
    tp_id = lax.axis_index("tp")
    ids = jnp.stack([tp_id, section_id]).astype(jnp.int32)
    tok_blocks = [tokens[m * MB : (m + 1) * MB] for m in range(MICRO)]
    cot_blocks = [cotangent[m * MB : (m + 1) * MB] for m in range(MICRO)]
    weights = gather_weights(master[0].astype(BF16)).reshape(2, HALF, HALF)

    stash = []
    own = tok_blocks[0]
    for tick in range(TICKS):
        other = swap_cores(own)
        following = tok_blocks[min(tick + 1, MICRO - 1)]
        send, preact, scale = forward_tick(ids, own, other, following, weights)
        stash.append((own, other, preact, scale))
        if tick < TICKS - 1:
            own = to_section(send, 1)

    grads, deltas = [None] * TICKS, [None] * TICKS
    grad = cot_blocks[MICRO - 1]
    for step in range(TICKS):
        tick = TICKS - 1 - step
        own, other, preact, scale = stash[tick]
        scaled, own_part, other_part = backward_tick(ids, grad, own, other, preact, scale, weights)
        received = swap_cores(other_part)
        grad_out = (grad.astype(F32) + own_part + received.astype(F32)).astype(BF16)
        grads[tick], deltas[tick] = grad_out, scaled
        if step < TICKS - 1:
            following = cot_blocks[max(MICRO - 2 - step, 0)]
            grad = to_section(jnp.where(section_id == 0, following, grad_out), -1)

    def live(blocks):
        return lax.dynamic_slice_in_dim(jnp.concatenate(blocks), section_id * MB, MICRO * MB, 0)

    own_all = live([entry[0] for entry in stash])
    other_all = live([entry[1] for entry in stash])
    delta_all = live(deltas)
    x_halves = [jnp.where(tp_id == h, own_all, other_all) for h in range(2)]
    x_all = jnp.concatenate(x_halves, axis=1)
    grad_rows = scatter_grads(
        lax.dot_general(
            x_all, delta_all, (((0,), (0,)), ((), ())), preferred_element_type=F32
        ).astype(BF16)
    ).astype(F32)
    updated = master[0] - STEP_SIZE * grad_rows / (MICRO * MB * island_count)
    return (live(grads)[None], updated[None])


def solution(mesh):
    placed = (P("island", "tp"), P("island", "tp"), P("section", "island", "tp"))
    return jax.shard_map(
        body,
        mesh=mesh,
        in_specs=placed,
        out_specs=(P("section", "island", "tp"), P("section", "island", "tp")),
        check_vma=False,
    )
```

```python
import functools

import jax
import jax.numpy as jnp
from jax import lax
from jax.experimental import pallas as pl
from jax.experimental.pallas import tpu as pltpu
from jax.sharding import PartitionSpec as P

D = 3584
HALF = 1792
MICRO = 4
MB = 48
SECTIONS = 8
ISLANDS = 16
SIDE = 4
ROWS = D // ISLANDS
FORWARD_TICKS = MICRO + SECTIONS - 1
TICKS = FORWARD_TICKS + SECTIONS
SPLIT = 1024
ROW_CHUNKS = (96, 128)
EARLY = 2
NORM_EPS = 1e-05
STEP_SIZE = 1.0
F32 = jnp.float32
BF16 = jnp.bfloat16
N_TILE = 256
K_TILE = 256
LIMIT_MB = 8
PARAMS = pltpu.CompilerParams(vmem_limit_bytes=LIMIT_MB * 1024 * 1024)
VMEM = pl.BlockSpec(memory_space=pltpu.VMEM)
SMEM = pl.BlockSpec(memory_space=pltpu.SMEM)


def half_rows(half, start, size):
    return pl.ds(pl.multiple_of(half * HALF + start, 256), size)


def slot_of(micro):
    return jnp.where((micro >= 0) & (micro < MICRO), micro, MICRO)


def backward_micro(tick, section):
    return tick - (2 * SECTIONS - 1) + section


def forward_kernel(
    tick, ids, own, other, next_tokens, weights_a, weights_b, _x, _pre, _scale, send, x_slots, preacts, scales
):
    tp_id = ids[0]
    is_last = ids[1] == SECTIONS - 1
    slot = slot_of(tick - ids[1])
    x_slots[slot, tp_id] = own[...]
    x_slots[slot, 1 - tp_id] = other[...]
    own_float = own[...].astype(F32)
    other_float = other[...].astype(F32)
    square_sum = jnp.sum(own_float * own_float, axis=1, keepdims=True)
    square_sum += jnp.sum(other_float * other_float, axis=1, keepdims=True)
    row_scale = lax.rsqrt(square_sum / D + NORM_EPS)
    scales[slot] = jnp.broadcast_to(row_scale, scales.shape[1:])
    for start in range(0, HALF, N_TILE):
        cols = pl.ds(start, N_TILE)
        weights = weights_a if start < SPLIT else weights_b
        part = pl.ds(start if start < SPLIT else start - SPLIT, N_TILE)
        product = jnp.dot(
            own[...], weights[half_rows(tp_id, 0, HALF), part], preferred_element_type=F32
        )
        product += jnp.dot(
            other[...], weights[half_rows(1 - tp_id, 0, HALF), part], preferred_element_type=F32
        )
        value = product * row_scale
        preacts[slot, :, cols] = value
        output = own[:, cols].astype(F32) + value / (1.0 + jnp.exp(-value))
        output = output.astype(BF16).astype(F32)
        send[:, cols] = jnp.where(is_last, next_tokens[:, cols].astype(F32), output).astype(BF16)


def shape_of(value):
    return jax.ShapeDtypeStruct(value.shape, value.dtype)


def forward_tick(tick, ids, own, other, next_tokens, weights, stash):
    return pl.pallas_call(
        functools.partial(forward_kernel, tick),
        out_shape=(shape_of(own), *map(shape_of, stash)),
        in_specs=[SMEM] + [VMEM] * 8,
        out_specs=(VMEM,) * 4,
        input_output_aliases={6: 1, 7: 2, 8: 3},
        compiler_params=PARAMS,
        cost_estimate=pl.CostEstimate(
            flops=2 * MB * D * HALF, bytes_accessed=2 * D * HALF, transcendentals=MB * HALF
        ),
        name="forward_tick",
    )(ids, own, other, next_tokens, *weights, *stash)


def backward_kernel(
    tick, ids, grad, x_slots, preacts, scales, weights_a, weights_b, _, own_part, other_part, deltas, scaled
):
    tp_id = ids[0]
    slot = slot_of(backward_micro(tick, ids[1]))
    row_scale = scales[slot, :, :1]
    mean_prod = jnp.zeros((MB, 1), F32)
    for start in range(0, HALF, N_TILE):
        cols = pl.ds(start, N_TILE)
        value = preacts[slot, :, cols]
        sig_value = 1.0 / (1.0 + jnp.exp(-value))
        delta = grad[:, cols].astype(F32) * (sig_value * (1.0 + value * (1.0 - sig_value)))
        mean_prod += jnp.sum(delta * value, axis=1, keepdims=True)
        scaled[:, cols] = (delta * row_scale).astype(BF16)
    shift = row_scale * row_scale * (mean_prod / D)
    deltas[slot] = scaled[...]
    across = (((1,), (1,)), ((), ()))
    for start in range(0, HALF, K_TILE):
        cols = pl.ds(start, K_TILE)
        for half, out in ((1 - tp_id, other_part), (tp_id, own_part)):
            rows = half_rows(half, start, K_TILE)
            product = lax.dot_general(
                scaled[:, :SPLIT], weights_a[rows, :], across, preferred_element_type=F32
            )
            product += lax.dot_general(
                scaled[:, SPLIT:], weights_b[rows, :], across, preferred_element_type=F32
            )
            product -= x_slots[slot, half, :, cols].astype(F32) * shift
            out[:, cols] = product.astype(out.dtype)


def backward_tick(tick, ids, grad, stash, weights, deltas):
    return pl.pallas_call(
        functools.partial(backward_kernel, tick),
        out_shape=(
            jax.ShapeDtypeStruct((MB, HALF), F32),
            jax.ShapeDtypeStruct((MB, HALF), BF16),
            shape_of(deltas),
        ),
        in_specs=[SMEM] + [VMEM] * 7,
        out_specs=(VMEM,) * 3,
        scratch_shapes=[pltpu.VMEM((MB, HALF), BF16)],
        input_output_aliases={7: 2},
        compiler_params=PARAMS,
        cost_estimate=pl.CostEstimate(
            flops=2 * MB * D * HALF, bytes_accessed=2 * D * HALF, transcendentals=MB * HALF
        ),
        name="backward_tick",
    )(ids, grad, *stash, *weights, deltas)


def swap_cores(value):
    return lax.ppermute(value, "tp", [(0, 1), (1, 0)])


def to_section(value, step):
    return lax.ppermute(value, "section", [(s, (s + step) % SECTIONS) for s in range(SECTIONS)])


def along_y(value, step):
    pairs = [(i, (i // SIDE + step) % SIDE * SIDE + i % SIDE) for i in range(ISLANDS)]
    return lax.ppermute(value, "island", pairs)


def along_z(value, step):
    pairs = [(i, i // SIDE * SIDE + (i % SIDE + step) % SIDE) for i in range(ISLANDS)]
    return lax.ppermute(value, "island", pairs)


def ring_gather(block, shift, place, target, at):
    half = block.shape[0] // 2
    below, above = shift(block, 1), shift(block, -1)
    far_low, far_high = shift(below[:half], 1), shift(above[half:], -1)
    target = at(target, place, block, 0)
    target = at(target, (place + SIDE - 1) % SIDE, below, 0)
    target = at(target, (place + 1) % SIDE, above, 0)
    target = at(target, (place + 2) % SIDE, far_low, 0)
    return at(target, (place + 2) % SIDE, far_high, half)


def gather_islands(block, target, row_start):
    island = lax.axis_index("island")
    y_place, z_place = island // SIDE, island % SIDE
    tail = (1,) * (target.ndim - 4)

    def at_z(buffer, position, piece, start):
        return lax.dynamic_update_slice(buffer, piece[None], (position, start, 0))

    def at_y(buffer, position, piece, start):
        piece = piece.reshape(1, *piece.shape[:1], *tail, *piece.shape[1:])
        return lax.dynamic_update_slice(
            buffer, piece, (position, start, row_start) + (0,) * (buffer.ndim - 3)
        )

    column = ring_gather(block, along_z, z_place, jnp.zeros((SIDE, *block.shape), BF16), at_z)
    return ring_gather(column, along_y, y_place, target, at_y)


def gather_weights(rows):
    by_gather = lax.all_gather(rows[:, :SPLIT], "island", axis=0, tiled=True)
    by_rings = jnp.zeros((SIDE, SIDE, ROWS, HALF - SPLIT), BF16)
    start = 0
    for size in ROW_CHUNKS:
        block = rows[start : start + size, SPLIT:]
        by_rings = gather_islands(block, by_rings, start)
        start += size
    return by_gather, by_rings.reshape(D, HALF - SPLIT)


def body(tokens, cotangent, master):
    island_count = lax.axis_size("island")
    section_id = lax.axis_index("section")
    tp_id = lax.axis_index("tp")
    ids = jnp.stack([tp_id, section_id]).astype(jnp.int32)
    tok_blocks = [tokens[m * MB : (m + 1) * MB] for m in range(MICRO)]
    cot_blocks = [cotangent[m * MB : (m + 1) * MB] for m in range(MICRO)]
    weights = gather_weights(master[0].astype(BF16))

    stash = (
        jnp.zeros((MICRO + 1, 2, MB, HALF), BF16),
        jnp.zeros((MICRO + 1, MB, HALF), F32),
        jnp.zeros((MICRO + 1, MB, 128), F32),
    )
    deltas = jnp.zeros((MICRO + 1, MB, HALF), BF16)
    grads = jnp.zeros((MICRO + 1, MB, HALF), BF16)
    ring_deltas = jnp.zeros((SIDE, SIDE, MICRO - EARLY, MB, HALF), BF16)
    own, grad = tok_blocks[0], cot_blocks[0]
    for tick in range(TICKS):
        if tick < FORWARD_TICKS:
            other = swap_cores(own)
            following = tok_blocks[min(tick + 1, MICRO - 1)]
            send, *stash = forward_tick(tick, ids, own, other, following, weights, stash)
            if tick < FORWARD_TICKS - 1:
                own = to_section(send, 1)
        if tick >= SECTIONS:
            own_part, other_part, deltas = backward_tick(
                tick, ids, grad, stash, weights, deltas
            )
            received = swap_cores(other_part)
            grad_out = (grad.astype(F32) + own_part + received.astype(F32)).astype(BF16)
            slot = slot_of(backward_micro(tick, section_id))
            grads = lax.dynamic_update_slice_in_dim(grads, grad_out[None], slot, 0)
            if tick < TICKS - 1:
                following = cot_blocks[min(tick + 1 - SECTIONS, MICRO - 1)]
                grad = to_section(jnp.where(section_id == 0, following, grad_out), -1)
        micro = tick - (2 * SECTIONS - 1)
        if micro == EARLY - 1:
            early_deltas = lax.all_gather(deltas[:EARLY], "island")
        elif micro >= EARLY:
            ring_deltas = gather_islands(deltas[micro], ring_deltas, micro - EARLY)

    core_micros = MICRO // 2
    x_part = lax.dynamic_slice_in_dim(stash[0], tp_id * core_micros, core_micros, 0)
    x_part = x_part.reshape(core_micros, 2, MB, ISLANDS // 2, ROWS).transpose(1, 3, 0, 2, 4)
    x_part = x_part.reshape(ISLANDS, core_micros * MB, ROWS)
    x_part = lax.all_to_all(x_part, "island", 0, 0)
    x_other = swap_cores(x_part)

    def outer(x_rows, delta_rows):
        return lax.dot_general(
            x_rows.reshape(-1, ROWS),
            delta_rows.reshape(-1, HALF),
            (((0,), (0,)), ((), ())),
            preferred_element_type=F32,
        )

    late_rows = outer(jnp.where(tp_id == 1, x_part, x_other), ring_deltas)
    late_rows = lax.optimization_barrier(late_rows)
    grad_rows = late_rows + outer(jnp.where(tp_id == 0, x_part, x_other), early_deltas)
    updated = master[0] - STEP_SIZE * grad_rows / (MICRO * MB * island_count)
    return (grads[:MICRO].reshape(1, MICRO * MB, HALF), updated[None])


def solution(mesh):
    placed = (P("island", "tp"), P("island", "tp"), P("section", "island", "tp"))
    return jax.shard_map(
        body,
        mesh=mesh,
        in_specs=placed,
        out_specs=(P("section", "island", "tp"), P("section", "island", "tp")),
        check_vma=False,
    )
```

```python
import functools

import jax
import jax.numpy as jnp
from jax import lax
from jax.experimental import pallas as pl
from jax.experimental.pallas import tpu as pltpu
from jax.sharding import PartitionSpec as P

D = 3584
HALF = 1792
MICRO = 4
MB = 48
SECTIONS = 8
ISLANDS = 16
SIDE = 4
ROWS = D // ISLANDS
FORWARD_TICKS = MICRO + SECTIONS - 1
TICKS = FORWARD_TICKS + SECTIONS
SPLIT = 1024
ROW_CHUNKS = (96, 128)
EARLY = 2
NORM_EPS = 1e-05
STEP_SIZE = 1.0
F32 = jnp.float32
BF16 = jnp.bfloat16
N_TILE = 256
K_TILE = 256
LIMIT_MB = 8
PARAMS = pltpu.CompilerParams(vmem_limit_bytes=LIMIT_MB * 1024 * 1024)
VMEM = pl.BlockSpec(memory_space=pltpu.VMEM)
SMEM = pl.BlockSpec(memory_space=pltpu.SMEM)


def half_rows(half, start, size):
    return pl.ds(pl.multiple_of(half * HALF + start, 256), size)


def slot_of(micro):
    return jnp.where((micro >= 0) & (micro < MICRO), micro, MICRO)


def backward_micro(tick, section):
    return tick - (2 * SECTIONS - 1) + section


def forward_kernel(
    tick, first, ids, own, other, next_tokens, weights_a, weights_b, *refs
):
    send, x_slots, preacts, scales = refs if first else refs[3:]
    tp_id = ids[0]
    is_last = ids[1] == SECTIONS - 1
    slot = slot_of(tick - ids[1])
    x_slots[slot, tp_id] = own[...]
    x_slots[slot, 1 - tp_id] = other[...]
    own_float = own[...].astype(F32)
    other_float = other[...].astype(F32)
    square_sum = jnp.sum(own_float * own_float, axis=1, keepdims=True)
    square_sum += jnp.sum(other_float * other_float, axis=1, keepdims=True)
    row_scale = lax.rsqrt(square_sum / D + NORM_EPS)
    scales[slot] = jnp.broadcast_to(row_scale, scales.shape[1:])
    for start in range(0, HALF, N_TILE):
        cols = pl.ds(start, N_TILE)
        weights = weights_a if start < SPLIT else weights_b
        part = pl.ds(start if start < SPLIT else start - SPLIT, N_TILE)
        product = jnp.dot(
            own[...], weights[half_rows(tp_id, 0, HALF), part], preferred_element_type=F32
        )
        product += jnp.dot(
            other[...], weights[half_rows(1 - tp_id, 0, HALF), part], preferred_element_type=F32
        )
        value = product * row_scale
        preacts[slot, :, cols] = value
        output = own[:, cols].astype(F32) + value / (1.0 + jnp.exp(-value))
        output = output.astype(BF16).astype(F32)
        send[:, cols] = jnp.where(is_last, next_tokens[:, cols].astype(F32), output).astype(BF16)


STASH = (
    jax.ShapeDtypeStruct((MICRO + 1, 2, MB, HALF), BF16),
    jax.ShapeDtypeStruct((MICRO + 1, MB, HALF), F32),
    jax.ShapeDtypeStruct((MICRO + 1, MB, 128), F32),
)


def forward_tick(tick, ids, own, other, next_tokens, weights, stash):
    first = not stash
    return pl.pallas_call(
        functools.partial(forward_kernel, tick, first),
        out_shape=(jax.ShapeDtypeStruct(own.shape, BF16), *STASH),
        in_specs=[SMEM] + [VMEM] * (5 + len(stash)),
        out_specs=(VMEM,) * 4,
        input_output_aliases={} if first else {6: 1, 7: 2, 8: 3},
        compiler_params=PARAMS,
        cost_estimate=pl.CostEstimate(
            flops=2 * MB * D * HALF, bytes_accessed=2 * D * HALF, transcendentals=MB * HALF
        ),
        name="forward_tick",
    )(ids, own, other, next_tokens, *weights, *stash)


def backward_kernel(
    tick, first, ids, grad, x_slots, preacts, scales, weights_a, weights_b, *refs
):
    own_part, other_part, deltas, scaled = refs if first else refs[1:]
    tp_id = ids[0]
    slot = slot_of(backward_micro(tick, ids[1]))
    row_scale = scales[slot, :, :1]
    mean_prod = jnp.zeros((MB, 1), F32)
    for start in range(0, HALF, N_TILE):
        cols = pl.ds(start, N_TILE)
        value = preacts[slot, :, cols]
        sig_value = 1.0 / (1.0 + jnp.exp(-value))
        delta = grad[:, cols].astype(F32) * (sig_value * (1.0 + value * (1.0 - sig_value)))
        mean_prod += jnp.sum(delta * value, axis=1, keepdims=True)
        scaled[:, cols] = (delta * row_scale).astype(BF16)
    shift = row_scale * row_scale * (mean_prod / D)
    deltas[slot] = scaled[...]
    across = (((1,), (1,)), ((), ()))
    for start in range(0, HALF, K_TILE):
        cols = pl.ds(start, K_TILE)
        for half, out in ((1 - tp_id, other_part), (tp_id, own_part)):
            rows = half_rows(half, start, K_TILE)
            product = lax.dot_general(
                scaled[:, :SPLIT], weights_a[rows, :], across, preferred_element_type=F32
            )
            product += lax.dot_general(
                scaled[:, SPLIT:], weights_b[rows, :], across, preferred_element_type=F32
            )
            product -= x_slots[slot, half, :, cols].astype(F32) * shift
            out[:, cols] = product.astype(out.dtype)


def backward_tick(tick, ids, grad, stash, weights, deltas):
    first = not deltas
    return pl.pallas_call(
        functools.partial(backward_kernel, tick, first),
        out_shape=(
            jax.ShapeDtypeStruct((MB, HALF), F32),
            jax.ShapeDtypeStruct((MB, HALF), BF16),
            jax.ShapeDtypeStruct((MICRO + 1, MB, HALF), BF16),
        ),
        in_specs=[SMEM] + [VMEM] * (6 + len(deltas)),
        out_specs=(VMEM,) * 3,
        scratch_shapes=[pltpu.VMEM((MB, HALF), BF16)],
        input_output_aliases={} if first else {7: 2},
        compiler_params=PARAMS,
        cost_estimate=pl.CostEstimate(
            flops=2 * MB * D * HALF, bytes_accessed=2 * D * HALF, transcendentals=MB * HALF
        ),
        name="backward_tick",
    )(ids, grad, *stash, *weights, *deltas)


def swap_cores(value):
    return lax.ppermute(value, "tp", [(0, 1), (1, 0)])


def to_section(value, step):
    return lax.ppermute(value, "section", [(s, (s + step) % SECTIONS) for s in range(SECTIONS)])


def along_y(value, step):
    pairs = [(i, (i // SIDE + step) % SIDE * SIDE + i % SIDE) for i in range(ISLANDS)]
    return lax.ppermute(value, "island", pairs)


def along_z(value, step):
    pairs = [(i, i // SIDE * SIDE + (i % SIDE + step) % SIDE) for i in range(ISLANDS)]
    return lax.ppermute(value, "island", pairs)


def ring_gather(block, shift, place, target, at):
    half = block.shape[0] // 2
    below, above = shift(block, 1), shift(block, -1)
    far_low, far_high = shift(below[:half], 1), shift(above[half:], -1)
    target = at(target, place, block, 0)
    target = at(target, (place + SIDE - 1) % SIDE, below, 0)
    target = at(target, (place + 1) % SIDE, above, 0)
    target = at(target, (place + 2) % SIDE, far_low, 0)
    return at(target, (place + 2) % SIDE, far_high, half)


def gather_islands(block, target, row_start):
    island = lax.axis_index("island")
    y_place, z_place = island // SIDE, island % SIDE
    tail = (1,) * (target.ndim - 4)

    def at_z(buffer, position, piece, start):
        return lax.dynamic_update_slice(buffer, piece[None], (position, start, 0))

    def at_y(buffer, position, piece, start):
        piece = piece.reshape(1, *piece.shape[:1], *tail, *piece.shape[1:])
        return lax.dynamic_update_slice(
            buffer, piece, (position, start, row_start) + (0,) * (buffer.ndim - 3)
        )

    column = ring_gather(block, along_z, z_place, jnp.zeros((SIDE, *block.shape), BF16), at_z)
    return ring_gather(column, along_y, y_place, target, at_y)


def gather_weights(rows):
    by_gather = lax.all_gather(rows[:, :SPLIT], "island", axis=0, tiled=True)
    by_rings = jnp.zeros((SIDE, SIDE, ROWS, HALF - SPLIT), BF16)
    start = 0
    for size in ROW_CHUNKS:
        block = rows[start : start + size, SPLIT:]
        by_rings = gather_islands(block, by_rings, start)
        start += size
    return by_gather, by_rings.reshape(D, HALF - SPLIT)


def body(tokens, cotangent, master):
    island_count = lax.axis_size("island")
    section_id = lax.axis_index("section")
    tp_id = lax.axis_index("tp")
    ids = jnp.stack([tp_id, section_id]).astype(jnp.int32)
    tok_blocks = [tokens[m * MB : (m + 1) * MB] for m in range(MICRO)]
    cot_blocks = [cotangent[m * MB : (m + 1) * MB] for m in range(MICRO)]
    weights = gather_weights(master[0].astype(BF16))

    tok_blocks, cot_blocks = lax.optimization_barrier((tok_blocks, cot_blocks))
    stash, deltas = (), None
    grads = jnp.zeros((MICRO + 1, MB, HALF), BF16)
    own, grad = tok_blocks[0], cot_blocks[0]
    for tick in range(TICKS):
        if tick < FORWARD_TICKS:
            other = swap_cores(own)
            following = tok_blocks[min(tick + 1, MICRO - 1)]
            send, *stash = forward_tick(tick, ids, own, other, following, weights, stash)
            if tick < FORWARD_TICKS - 1:
                own = to_section(send, 1)
        if tick >= SECTIONS:
            own_part, other_part, deltas = backward_tick(
                tick, ids, grad, stash, weights, () if deltas is None else (deltas,)
            )
            received = swap_cores(other_part)
            grad_out = (grad.astype(F32) + own_part + received.astype(F32)).astype(BF16)
            slot = slot_of(backward_micro(tick, section_id))
            grads = lax.dynamic_update_slice_in_dim(grads, grad_out[None], slot, 0)
            if tick < TICKS - 1:
                following = cot_blocks[min(tick + 1 - SECTIONS, MICRO - 1)]
                grad = to_section(jnp.where(section_id == 0, following, grad_out), -1)
        micro = tick - (2 * SECTIONS - 1)
        if micro == EARLY - 1:
            early_deltas = lax.all_gather(deltas[:EARLY], "island")

    x_slots, deltas, empty = lax.optimization_barrier((stash[0], deltas, jnp.zeros((), BF16)))
    ring_deltas = jnp.broadcast_to(empty, (SIDE, SIDE, MICRO - EARLY, MB, HALF))
    for micro in range(EARLY, MICRO):
        ring_deltas = gather_islands(deltas[micro], ring_deltas, micro - EARLY)

    core_micros = MICRO // 2
    x_part = lax.dynamic_slice_in_dim(x_slots, tp_id * core_micros, core_micros, 0)
    x_part = x_part.reshape(core_micros, 2, MB, ISLANDS // 2, ROWS).transpose(1, 3, 0, 2, 4)
    x_part = x_part.reshape(ISLANDS, core_micros * MB, ROWS)
    x_part = lax.all_to_all(x_part, "island", 0, 0)
    x_other = swap_cores(x_part)

    def outer(x_rows, delta_rows):
        return lax.dot_general(
            x_rows.reshape(-1, ROWS),
            delta_rows.reshape(-1, HALF),
            (((0,), (0,)), ((), ())),
            preferred_element_type=F32,
        )

    late_rows = outer(jnp.where(tp_id == 1, x_part, x_other), ring_deltas)
    late_rows = lax.optimization_barrier(late_rows)
    grad_rows = late_rows + outer(jnp.where(tp_id == 0, x_part, x_other), early_deltas)
    updated = master[0] - STEP_SIZE * grad_rows / (MICRO * MB * island_count)
    return (grads[:MICRO].reshape(1, MICRO * MB, HALF), updated[None])


def solution(mesh):
    placed = (P("island", "tp"), P("island", "tp"), P("section", "island", "tp"))
    return jax.shard_map(
        body,
        mesh=mesh,
        in_specs=placed,
        out_specs=(P("section", "island", "tp"), P("section", "island", "tp")),
        check_vma=False,
    )
```

```python
import functools

import jax
import jax.numpy as jnp
from jax import lax
from jax.experimental import pallas as pl
from jax.experimental.pallas import tpu as pltpu
from jax.sharding import PartitionSpec as P

D = 3584
HALF = 1792
MICRO = 4
MB = 48
SECTIONS = 8
ISLANDS = 16
SIDE = 4
ROWS = D // ISLANDS
FORWARD_TICKS = MICRO + SECTIONS - 1
TICKS = FORWARD_TICKS + SECTIONS
SPLIT = 768
ROW_CHUNKS = (96, 128)
EARLY = 2
NORM_EPS = 1e-05
STEP_SIZE = 1.0
F32 = jnp.float32
BF16 = jnp.bfloat16
N_TILE = 256
K_TILE = 256
LIMIT_MB = 8
PARAMS = pltpu.CompilerParams(vmem_limit_bytes=LIMIT_MB * 1024 * 1024)
VMEM = pl.BlockSpec(memory_space=pltpu.VMEM)
SMEM = pl.BlockSpec(memory_space=pltpu.SMEM)


def half_rows(half, start, size):
    return pl.ds(pl.multiple_of(half * HALF + start, 256), size)


def slot_of(micro):
    return jnp.where((micro >= 0) & (micro < MICRO), micro, MICRO)


def backward_micro(tick, section):
    return tick - (2 * SECTIONS - 1) + section


def forward_kernel(
    tick, first, ids, own, other, next_tokens, weights_a, weights_b, *refs
):
    send, x_slots, preacts, scales = refs if first else refs[3:]
    tp_id = ids[0]
    is_last = ids[1] == SECTIONS - 1
    slot = slot_of(tick - ids[1])
    x_slots[slot, tp_id] = own[...]
    x_slots[slot, 1 - tp_id] = other[...]
    own_float = own[...].astype(F32)
    other_float = other[...].astype(F32)
    square_sum = jnp.sum(own_float * own_float, axis=1, keepdims=True)
    square_sum += jnp.sum(other_float * other_float, axis=1, keepdims=True)
    row_scale = lax.rsqrt(square_sum / D + NORM_EPS)
    scales[slot] = jnp.broadcast_to(row_scale, scales.shape[1:])
    for start in range(0, HALF, N_TILE):
        cols = pl.ds(start, N_TILE)
        weights = weights_a if start < SPLIT else weights_b
        part = pl.ds(start if start < SPLIT else start - SPLIT, N_TILE)
        product = jnp.dot(
            own[...], weights[half_rows(tp_id, 0, HALF), part], preferred_element_type=F32
        )
        product += jnp.dot(
            other[...], weights[half_rows(1 - tp_id, 0, HALF), part], preferred_element_type=F32
        )
        value = product * row_scale
        preacts[slot, :, cols] = value
        output = own[:, cols].astype(F32) + value / (1.0 + jnp.exp(-value))
        output = output.astype(BF16).astype(F32)
        send[:, cols] = jnp.where(is_last, next_tokens[:, cols].astype(F32), output).astype(BF16)


STASH = (
    jax.ShapeDtypeStruct((MICRO + 1, 2, MB, HALF), BF16),
    jax.ShapeDtypeStruct((MICRO + 1, MB, HALF), F32),
    jax.ShapeDtypeStruct((MICRO + 1, MB, 128), F32),
)


def forward_tick(tick, ids, own, other, next_tokens, weights, stash):
    first = not stash
    return pl.pallas_call(
        functools.partial(forward_kernel, tick, first),
        out_shape=(jax.ShapeDtypeStruct(own.shape, BF16), *STASH),
        in_specs=[SMEM] + [VMEM] * (5 + len(stash)),
        out_specs=(VMEM,) * 4,
        input_output_aliases={} if first else {6: 1, 7: 2, 8: 3},
        compiler_params=PARAMS,
        cost_estimate=pl.CostEstimate(
            flops=2 * MB * D * HALF, bytes_accessed=2 * D * HALF, transcendentals=MB * HALF
        ),
        name="forward_tick",
    )(ids, own, other, next_tokens, *weights, *stash)


def backward_kernel(
    tick, first, ids, grad, x_slots, preacts, scales, weights_a, weights_b, *refs
):
    own_part, other_part, deltas, scaled = refs if first else refs[1:]
    tp_id = ids[0]
    slot = slot_of(backward_micro(tick, ids[1]))
    row_scale = scales[slot, :, :1]
    mean_prod = jnp.zeros((MB, 1), F32)
    for start in range(0, HALF, N_TILE):
        cols = pl.ds(start, N_TILE)
        value = preacts[slot, :, cols]
        sig_value = 1.0 / (1.0 + jnp.exp(-value))
        delta = grad[:, cols].astype(F32) * (sig_value * (1.0 + value * (1.0 - sig_value)))
        mean_prod += jnp.sum(delta * value, axis=1, keepdims=True)
        scaled[:, cols] = (delta * row_scale).astype(BF16)
    shift = row_scale * row_scale * (mean_prod / D)
    deltas[slot] = scaled[...]
    across = (((1,), (1,)), ((), ()))
    for start in range(0, HALF, K_TILE):
        cols = pl.ds(start, K_TILE)
        for half, out in ((1 - tp_id, other_part), (tp_id, own_part)):
            rows = half_rows(half, start, K_TILE)
            product = lax.dot_general(
                scaled[:, :SPLIT], weights_a[rows, :], across, preferred_element_type=F32
            )
            product += lax.dot_general(
                scaled[:, SPLIT:], weights_b[rows, :], across, preferred_element_type=F32
            )
            product -= x_slots[slot, half, :, cols].astype(F32) * shift
            out[:, cols] = product.astype(out.dtype)


def backward_tick(tick, ids, grad, stash, weights, deltas):
    first = not deltas
    return pl.pallas_call(
        functools.partial(backward_kernel, tick, first),
        out_shape=(
            jax.ShapeDtypeStruct((MB, HALF), F32),
            jax.ShapeDtypeStruct((MB, HALF), BF16),
            jax.ShapeDtypeStruct((MICRO + 1, MB, HALF), BF16),
        ),
        in_specs=[SMEM] + [VMEM] * (6 + len(deltas)),
        out_specs=(VMEM,) * 3,
        scratch_shapes=[pltpu.VMEM((MB, HALF), BF16)],
        input_output_aliases={} if first else {7: 2},
        compiler_params=PARAMS,
        cost_estimate=pl.CostEstimate(
            flops=2 * MB * D * HALF, bytes_accessed=2 * D * HALF, transcendentals=MB * HALF
        ),
        name="backward_tick",
    )(ids, grad, *stash, *weights, *deltas)


def swap_cores(value):
    return lax.ppermute(value, "tp", [(0, 1), (1, 0)])


def to_section(value, step):
    return lax.ppermute(value, "section", [(s, (s + step) % SECTIONS) for s in range(SECTIONS)])


def along_y(value, step):
    pairs = [(i, (i // SIDE + step) % SIDE * SIDE + i % SIDE) for i in range(ISLANDS)]
    return lax.ppermute(value, "island", pairs)


def along_z(value, step):
    pairs = [(i, i // SIDE * SIDE + (i % SIDE + step) % SIDE) for i in range(ISLANDS)]
    return lax.ppermute(value, "island", pairs)


def ring_gather(block, shift, place, target, at):
    half = block.shape[0] // 2
    below, above = shift(block, 1), shift(block, -1)
    far_low, far_high = shift(below[:half], 1), shift(above[half:], -1)
    target = at(target, place, block, 0)
    target = at(target, (place + SIDE - 1) % SIDE, below, 0)
    target = at(target, (place + 1) % SIDE, above, 0)
    target = at(target, (place + 2) % SIDE, far_low, 0)
    return at(target, (place + 2) % SIDE, far_high, half)


def gather_islands(block, target, row_start):
    island = lax.axis_index("island")
    y_place, z_place = island // SIDE, island % SIDE
    tail = (1,) * (target.ndim - 4)

    def at_z(buffer, position, piece, start):
        return lax.dynamic_update_slice(buffer, piece[None], (position, start, 0))

    def at_y(buffer, position, piece, start):
        piece = piece.reshape(1, *piece.shape[:1], *tail, *piece.shape[1:])
        return lax.dynamic_update_slice(
            buffer, piece, (position, start, row_start) + (0,) * (buffer.ndim - 3)
        )

    column = ring_gather(block, along_z, z_place, jnp.zeros((SIDE, *block.shape), BF16), at_z)
    return ring_gather(column, along_y, y_place, target, at_y), column


def after(value, earlier):
    return value if earlier is None else lax.optimization_barrier((value, earlier))[0]


def gather_weights(rows):
    by_gather = lax.all_gather(rows[:, :SPLIT], "island", axis=0, tiled=True)
    by_rings = jnp.zeros((SIDE, SIDE, ROWS, HALF - SPLIT), BF16)
    start, column = 0, None
    for size in ROW_CHUNKS:
        block = after(rows[start : start + size, SPLIT:], column)
        by_rings, column = gather_islands(block, by_rings, start)
        start += size
    return by_gather, by_rings.reshape(D, HALF - SPLIT)


def exchange_x(x_slots, tp_id):
    count = MICRO // 2
    part = lax.dynamic_slice_in_dim(x_slots, tp_id * count, count, 0)
    part = part.reshape(count, 2, MB, ISLANDS // 2, ROWS).transpose(1, 3, 0, 2, 4)
    return lax.all_to_all(part.reshape(ISLANDS, count * MB, ROWS), "island", 0, 0)


def body(tokens, cotangent, master):
    island_count = lax.axis_size("island")
    section_id = lax.axis_index("section")
    tp_id = lax.axis_index("tp")
    ids = jnp.stack([tp_id, section_id]).astype(jnp.int32)
    tok_blocks = [tokens[m * MB : (m + 1) * MB] for m in range(MICRO)]
    cot_blocks = [cotangent[m * MB : (m + 1) * MB] for m in range(MICRO)]
    weights = gather_weights(master[0].astype(BF16))

    tok_blocks, cot_blocks = lax.optimization_barrier((tok_blocks, cot_blocks))
    stash, deltas = (), None
    grads = jnp.zeros((MICRO + 1, MB, HALF), BF16)
    own, grad = tok_blocks[0], cot_blocks[0]
    for tick in range(TICKS):
        if tick < FORWARD_TICKS:
            other = swap_cores(own)
            following = tok_blocks[min(tick + 1, MICRO - 1)]
            send, *stash = forward_tick(tick, ids, own, other, following, weights, stash)
            if tick < FORWARD_TICKS - 1:
                own = to_section(send, 1)
        if tick >= SECTIONS:
            own_part, other_part, deltas = backward_tick(
                tick, ids, grad, stash, weights, () if deltas is None else (deltas,)
            )
            received = swap_cores(other_part)
            grad_out = (grad.astype(F32) + own_part + received.astype(F32)).astype(BF16)
            slot = slot_of(backward_micro(tick, section_id))
            grads = lax.dynamic_update_slice_in_dim(grads, grad_out[None], slot, 0)
            if tick < TICKS - 1:
                following = cot_blocks[min(tick + 1 - SECTIONS, MICRO - 1)]
                passed = jnp.where(section_id == 0, following, grad_out)
                grad = to_section(passed, -1)
                if tick == FORWARD_TICKS:
                    x_part = exchange_x(after(stash[0], passed), tp_id)
                    grad = after(grad, x_part)
        micro = tick - (2 * SECTIONS - 1)
        if micro == EARLY - 1:
            early_deltas = lax.all_gather(deltas[:EARLY], "island")

    deltas, empty = lax.optimization_barrier((deltas, jnp.zeros((), BF16)))
    ring_deltas = jnp.broadcast_to(empty, (SIDE, SIDE, MICRO - EARLY, MB, HALF))
    column = None
    for micro in range(EARLY, MICRO):
        block = after(deltas[micro], column)
        ring_deltas, column = gather_islands(block, ring_deltas, micro - EARLY)

    x_other = swap_cores(x_part)

    def outer(x_rows, delta_rows):
        return lax.dot_general(
            x_rows.reshape(-1, ROWS),
            delta_rows.reshape(-1, HALF),
            (((0,), (0,)), ((), ())),
            preferred_element_type=F32,
        )

    early_rows = outer(jnp.where(tp_id == 0, x_part, x_other), early_deltas)
    early_rows = lax.optimization_barrier(early_rows)
    grad_rows = early_rows + outer(jnp.where(tp_id == 1, x_part, x_other), ring_deltas)
    updated = master[0] - STEP_SIZE * grad_rows / (MICRO * MB * island_count)
    return (grads[:MICRO].reshape(1, MICRO * MB, HALF), updated[None])


def solution(mesh):
    placed = (P("island", "tp"), P("island", "tp"), P("section", "island", "tp"))
    return jax.shard_map(
        body,
        mesh=mesh,
        in_specs=placed,
        out_specs=(P("section", "island", "tp"), P("section", "island", "tp")),
        check_vma=False,
    )
```

```python
import functools

import jax
import jax.numpy as jnp
from jax import lax
from jax.experimental import pallas as pl
from jax.experimental.pallas import tpu as pltpu
from jax.sharding import PartitionSpec as P

D = 3584
HALF = 1792
MICRO = 4
MB = 48
SECTIONS = 8
ISLANDS = 16
SIDE = 4
ROWS = D // ISLANDS
FORWARD_TICKS = MICRO + SECTIONS - 1
TICKS = FORWARD_TICKS + SECTIONS
SPLIT = 1024
ROW_CHUNKS = (96, 128)
EARLY = 2
NORM_EPS = 1e-05
STEP_SIZE = 1.0
F32 = jnp.float32
BF16 = jnp.bfloat16
N_TILE = 256
K_TILE = 256
LIMIT_MB = 8
PARAMS = pltpu.CompilerParams(vmem_limit_bytes=LIMIT_MB * 1024 * 1024)
VMEM = pl.BlockSpec(memory_space=pltpu.VMEM)
SMEM = pl.BlockSpec(memory_space=pltpu.SMEM)


def half_rows(half, start, size):
    return pl.ds(pl.multiple_of(half * HALF + start, 256), size)


def slot_of(micro):
    return jnp.where((micro >= 0) & (micro < MICRO), micro, MICRO)


def backward_micro(tick, section):
    return tick - (2 * SECTIONS - 1) + section


def forward_kernel(
    tick, first, ids, own, other, next_tokens, weights_a, weights_b, *refs
):
    send, x_slots, preacts, scales = refs if first else refs[3:]
    tp_id = ids[0]
    is_last = ids[1] == SECTIONS - 1
    slot = slot_of(tick - ids[1])
    x_slots[slot, tp_id] = own[...]
    x_slots[slot, 1 - tp_id] = other[...]
    own_float = own[...].astype(F32)
    other_float = other[...].astype(F32)
    square_sum = jnp.sum(own_float * own_float, axis=1, keepdims=True)
    square_sum += jnp.sum(other_float * other_float, axis=1, keepdims=True)
    row_scale = lax.rsqrt(square_sum / D + NORM_EPS)
    scales[slot] = jnp.broadcast_to(row_scale, scales.shape[1:])
    for start in range(0, HALF, N_TILE):
        cols = pl.ds(start, N_TILE)
        weights = weights_a if start < SPLIT else weights_b
        part = pl.ds(start if start < SPLIT else start - SPLIT, N_TILE)
        product = jnp.dot(
            own[...], weights[half_rows(tp_id, 0, HALF), part], preferred_element_type=F32
        )
        product += jnp.dot(
            other[...], weights[half_rows(1 - tp_id, 0, HALF), part], preferred_element_type=F32
        )
        value = product * row_scale
        preacts[slot, :, cols] = value
        output = own[:, cols].astype(F32) + value / (1.0 + jnp.exp(-value))
        output = output.astype(BF16).astype(F32)
        send[:, cols] = jnp.where(is_last, next_tokens[:, cols].astype(F32), output).astype(BF16)


STASH = (
    jax.ShapeDtypeStruct((MICRO + 1, 2, MB, HALF), BF16),
    jax.ShapeDtypeStruct((MICRO + 1, MB, HALF), F32),
    jax.ShapeDtypeStruct((MICRO + 1, MB, 128), F32),
)


def forward_tick(tick, ids, own, other, next_tokens, weights, stash):
    first = not stash
    return pl.pallas_call(
        functools.partial(forward_kernel, tick, first),
        out_shape=(jax.ShapeDtypeStruct(own.shape, BF16), *STASH),
        in_specs=[SMEM] + [VMEM] * (5 + len(stash)),
        out_specs=(VMEM,) * 4,
        input_output_aliases={} if first else {6: 1, 7: 2, 8: 3},
        compiler_params=PARAMS,
        cost_estimate=pl.CostEstimate(
            flops=2 * MB * D * HALF, bytes_accessed=2 * D * HALF, transcendentals=MB * HALF
        ),
        name="forward_tick",
    )(ids, own, other, next_tokens, *weights, *stash)


def backward_kernel(
    tick, first, ids, grad, x_slots, preacts, scales, weights_a, weights_b, *refs
):
    own_part, other_part, deltas, scaled = refs if first else refs[1:]
    tp_id = ids[0]
    slot = slot_of(backward_micro(tick, ids[1]))
    row_scale = scales[slot, :, :1]
    mean_prod = jnp.zeros((MB, 1), F32)
    for start in range(0, HALF, N_TILE):
        cols = pl.ds(start, N_TILE)
        value = preacts[slot, :, cols]
        sig_value = 1.0 / (1.0 + jnp.exp(-value))
        delta = grad[:, cols].astype(F32) * (sig_value * (1.0 + value * (1.0 - sig_value)))
        mean_prod += jnp.sum(delta * value, axis=1, keepdims=True)
        scaled[:, cols] = (delta * row_scale).astype(BF16)
    shift = row_scale * row_scale * (mean_prod / D)
    deltas[slot] = scaled[...]
    across = (((1,), (1,)), ((), ()))
    for start in range(0, HALF, K_TILE):
        cols = pl.ds(start, K_TILE)
        for half, out in ((1 - tp_id, other_part), (tp_id, own_part)):
            rows = half_rows(half, start, K_TILE)
            product = lax.dot_general(
                scaled[:, :SPLIT], weights_a[rows, :], across, preferred_element_type=F32
            )
            product += lax.dot_general(
                scaled[:, SPLIT:], weights_b[rows, :], across, preferred_element_type=F32
            )
            product -= x_slots[slot, half, :, cols].astype(F32) * shift
            out[:, cols] = product.astype(out.dtype)


def backward_tick(tick, ids, grad, stash, weights, deltas):
    first = not deltas
    return pl.pallas_call(
        functools.partial(backward_kernel, tick, first),
        out_shape=(
            jax.ShapeDtypeStruct((MB, HALF), F32),
            jax.ShapeDtypeStruct((MB, HALF), BF16),
            jax.ShapeDtypeStruct((MICRO + 1, MB, HALF), BF16),
        ),
        in_specs=[SMEM] + [VMEM] * (6 + len(deltas)),
        out_specs=(VMEM,) * 3,
        scratch_shapes=[pltpu.VMEM((MB, HALF), BF16)],
        input_output_aliases={} if first else {7: 2},
        compiler_params=PARAMS,
        cost_estimate=pl.CostEstimate(
            flops=2 * MB * D * HALF, bytes_accessed=2 * D * HALF, transcendentals=MB * HALF
        ),
        name="backward_tick",
    )(ids, grad, *stash, *weights, *deltas)


def swap_cores(value):
    return lax.ppermute(value, "tp", [(0, 1), (1, 0)])


def to_section(value, step):
    return lax.ppermute(value, "section", [(s, (s + step) % SECTIONS) for s in range(SECTIONS)])


def along_y(value, step):
    pairs = [(i, (i // SIDE + step) % SIDE * SIDE + i % SIDE) for i in range(ISLANDS)]
    return lax.ppermute(value, "island", pairs)


def along_z(value, step):
    pairs = [(i, i // SIDE * SIDE + (i % SIDE + step) % SIDE) for i in range(ISLANDS)]
    return lax.ppermute(value, "island", pairs)


def ring_gather(block, shift, place, target, at):
    half = block.shape[0] // 2
    below, above = shift(block, 1), shift(block, -1)
    far_low, far_high = shift(below[:half], 1), shift(above[half:], -1)
    target = at(target, place, block, 0)
    target = at(target, (place + SIDE - 1) % SIDE, below, 0)
    target = at(target, (place + 1) % SIDE, above, 0)
    target = at(target, (place + 2) % SIDE, far_low, 0)
    return at(target, (place + 2) % SIDE, far_high, half)


def gather_islands(block, target, row_start):
    island = lax.axis_index("island")
    y_place, z_place = island // SIDE, island % SIDE
    tail = (1,) * (target.ndim - 4)

    def at_z(buffer, position, piece, start):
        return lax.dynamic_update_slice(buffer, piece[None], (position, start, 0))

    def at_y(buffer, position, piece, start):
        piece = piece.reshape(1, *piece.shape[:1], *tail, *piece.shape[1:])
        return lax.dynamic_update_slice(
            buffer, piece, (position, start, row_start) + (0,) * (buffer.ndim - 3)
        )

    column = ring_gather(block, along_z, z_place, jnp.zeros((SIDE, *block.shape), BF16), at_z)
    return ring_gather(column, along_y, y_place, target, at_y), column


def after(value, earlier):
    return lax.optimization_barrier((value, earlier))[0]


def gather_weights(rows):
    by_gather = lax.all_gather(rows[:, :SPLIT], "island", axis=0, tiled=True)
    by_rings = jnp.zeros((SIDE, SIDE, ROWS, HALF - SPLIT), BF16)
    start = 0
    for size in ROW_CHUNKS:
        block = rows[start : start + size, SPLIT:]
        by_rings, _ = gather_islands(block, by_rings, start)
        start += size
    return by_gather, by_rings.reshape(D, HALF - SPLIT)


def exchange_x(x_slots, tp_id):
    count = MICRO // 2
    part = lax.dynamic_slice_in_dim(x_slots, tp_id * count, count, 0)
    part = part.reshape(count, 2, MB, ISLANDS // 2, ROWS).transpose(1, 3, 0, 2, 4)
    return lax.all_to_all(part.reshape(ISLANDS, count * MB, ROWS), "island", 0, 0)


def body(tokens, cotangent, master):
    island_count = lax.axis_size("island")
    section_id = lax.axis_index("section")
    tp_id = lax.axis_index("tp")
    ids = jnp.stack([tp_id, section_id]).astype(jnp.int32)
    tok_blocks = [tokens[m * MB : (m + 1) * MB] for m in range(MICRO)]
    cot_blocks = [cotangent[m * MB : (m + 1) * MB] for m in range(MICRO)]
    weights = gather_weights(master[0].astype(BF16))

    tok_blocks, cot_blocks = lax.optimization_barrier((tok_blocks, cot_blocks))
    stash, deltas = (), None
    grads = jnp.zeros((MICRO + 1, MB, HALF), BF16)
    own, grad = tok_blocks[0], cot_blocks[0]
    for tick in range(TICKS):
        if tick < FORWARD_TICKS:
            other = swap_cores(own)
            following = tok_blocks[min(tick + 1, MICRO - 1)]
            send, *stash = forward_tick(tick, ids, own, other, following, weights, stash)
            if tick < FORWARD_TICKS - 1:
                own = to_section(send, 1)
        if tick >= SECTIONS:
            own_part, other_part, deltas = backward_tick(
                tick, ids, grad, stash, weights, () if deltas is None else (deltas,)
            )
            received = swap_cores(other_part)
            grad_out = (grad.astype(F32) + own_part + received.astype(F32)).astype(BF16)
            slot = slot_of(backward_micro(tick, section_id))
            grads = lax.dynamic_update_slice_in_dim(grads, grad_out[None], slot, 0)
            if tick < TICKS - 1:
                following = cot_blocks[min(tick + 1 - SECTIONS, MICRO - 1)]
                passed = jnp.where(section_id == 0, following, grad_out)
                grad = to_section(passed, -1)
                if tick == TICKS - 2:
                    x_part = exchange_x(after(stash[0], passed), tp_id)
        micro = tick - (2 * SECTIONS - 1)
        if micro == EARLY - 1:
            early_deltas = lax.all_gather(deltas[:EARLY], "island")

    deltas, empty, x_part = lax.optimization_barrier((deltas, jnp.zeros((), BF16), x_part))
    ring_deltas = jnp.broadcast_to(empty, (SIDE, SIDE, MICRO - EARLY, MB, HALF))
    column = x_part
    for micro in range(EARLY, MICRO):
        block = after(deltas[micro], column)
        ring_deltas, column = gather_islands(block, ring_deltas, micro - EARLY)

    x_other = swap_cores(x_part)

    def outer(x_rows, delta_rows):
        return lax.dot_general(
            x_rows.reshape(-1, ROWS),
            delta_rows.reshape(-1, HALF),
            (((0,), (0,)), ((), ())),
            preferred_element_type=F32,
        )

    late_rows = outer(jnp.where(tp_id == 1, x_part, x_other), ring_deltas)
    late_rows = lax.optimization_barrier(late_rows)
    grad_rows = late_rows + outer(jnp.where(tp_id == 0, x_part, x_other), early_deltas)
    updated = master[0] - STEP_SIZE * grad_rows / (MICRO * MB * island_count)
    return (grads[:MICRO].reshape(1, MICRO * MB, HALF), updated[None])


def solution(mesh):
    placed = (P("island", "tp"), P("island", "tp"), P("section", "island", "tp"))
    return jax.shard_map(
        body,
        mesh=mesh,
        in_specs=placed,
        out_specs=(P("section", "island", "tp"), P("section", "island", "tp")),
        check_vma=False,
    )
```

```python
import functools

import jax
import jax.numpy as jnp
from jax import lax
from jax.experimental import pallas as pl
from jax.experimental.pallas import tpu as pltpu
from jax.sharding import PartitionSpec as P

D = 3584
HALF = 1792
MICRO = 4
MB = 48
SECTIONS = 8
ISLANDS = 16
SIDE = 4
ROWS = D // ISLANDS
FORWARD_TICKS = MICRO + SECTIONS - 1
TICKS = FORWARD_TICKS + SECTIONS
SPLIT = 1024
ROW_CHUNKS = (96, 128)
EARLY = 2
NORM_EPS = 1e-05
STEP_SIZE = 1.0
F32 = jnp.float32
BF16 = jnp.bfloat16
N_TILE = 256
K_TILE = 256
LIMIT_MB = 8
PARAMS = pltpu.CompilerParams(vmem_limit_bytes=LIMIT_MB * 1024 * 1024)
VMEM = pl.BlockSpec(memory_space=pltpu.VMEM)
SMEM = pl.BlockSpec(memory_space=pltpu.SMEM)


def half_rows(half, start, size):
    return pl.ds(pl.multiple_of(half * HALF + start, 256), size)


def slot_of(micro):
    return jnp.where((micro >= 0) & (micro < MICRO), micro, MICRO)


def backward_micro(tick, section):
    return tick - (2 * SECTIONS - 1) + section


def forward_kernel(
    tick, first, ids, own, other, next_tokens, weights_a, weights_b, *refs
):
    send, x_slots, preacts, scales = refs if first else refs[3:]
    tp_id = ids[0]
    is_last = ids[1] == SECTIONS - 1
    slot = slot_of(tick - ids[1])
    x_slots[slot, tp_id] = own[...]
    x_slots[slot, 1 - tp_id] = other[...]
    own_float = own[...].astype(F32)
    other_float = other[...].astype(F32)
    square_sum = jnp.sum(own_float * own_float, axis=1, keepdims=True)
    square_sum += jnp.sum(other_float * other_float, axis=1, keepdims=True)
    row_scale = lax.rsqrt(square_sum / D + NORM_EPS)
    scales[slot] = jnp.broadcast_to(row_scale, scales.shape[1:])
    for start in range(0, HALF, N_TILE):
        cols = pl.ds(start, N_TILE)
        weights = weights_a if start < SPLIT else weights_b
        part = pl.ds(start if start < SPLIT else start - SPLIT, N_TILE)
        product = jnp.dot(
            own[...], weights[half_rows(tp_id, 0, HALF), part], preferred_element_type=F32
        )
        product += jnp.dot(
            other[...], weights[half_rows(1 - tp_id, 0, HALF), part], preferred_element_type=F32
        )
        value = product * row_scale
        preacts[slot, :, cols] = value
        output = own[:, cols].astype(F32) + value / (1.0 + jnp.exp(-value))
        output = output.astype(BF16).astype(F32)
        send[:, cols] = jnp.where(is_last, next_tokens[:, cols].astype(F32), output).astype(BF16)


STASH = (
    jax.ShapeDtypeStruct((MICRO + 1, 2, MB, HALF), BF16),
    jax.ShapeDtypeStruct((MICRO + 1, MB, HALF), F32),
    jax.ShapeDtypeStruct((MICRO + 1, MB, 128), F32),
)


def forward_tick(tick, ids, own, other, next_tokens, weights, stash):
    first = not stash
    return pl.pallas_call(
        functools.partial(forward_kernel, tick, first),
        out_shape=(jax.ShapeDtypeStruct(own.shape, BF16), *STASH),
        in_specs=[SMEM] + [VMEM] * (5 + len(stash)),
        out_specs=(VMEM,) * 4,
        input_output_aliases={} if first else {6: 1, 7: 2, 8: 3},
        compiler_params=PARAMS,
        cost_estimate=pl.CostEstimate(
            flops=2 * MB * D * HALF, bytes_accessed=2 * D * HALF, transcendentals=MB * HALF
        ),
        name="forward_tick",
    )(ids, own, other, next_tokens, *weights, *stash)


def backward_kernel(
    tick, first, ids, grad, x_slots, preacts, scales, weights_a, weights_b, *refs
):
    own_part, other_part, deltas, scaled = refs if first else refs[1:]
    tp_id = ids[0]
    slot = slot_of(backward_micro(tick, ids[1]))
    row_scale = scales[slot, :, :1]
    mean_prod = jnp.zeros((MB, 1), F32)
    for start in range(0, HALF, N_TILE):
        cols = pl.ds(start, N_TILE)
        value = preacts[slot, :, cols]
        sig_value = 1.0 / (1.0 + jnp.exp(-value))
        delta = grad[:, cols].astype(F32) * (sig_value * (1.0 + value * (1.0 - sig_value)))
        mean_prod += jnp.sum(delta * value, axis=1, keepdims=True)
        scaled[:, cols] = (delta * row_scale).astype(BF16)
    shift = row_scale * row_scale * (mean_prod / D)
    deltas[slot] = scaled[...]
    across = (((1,), (1,)), ((), ()))
    for start in range(0, HALF, K_TILE):
        cols = pl.ds(start, K_TILE)
        for half, out in ((1 - tp_id, other_part), (tp_id, own_part)):
            rows = half_rows(half, start, K_TILE)
            product = lax.dot_general(
                scaled[:, :SPLIT], weights_a[rows, :], across, preferred_element_type=F32
            )
            product += lax.dot_general(
                scaled[:, SPLIT:], weights_b[rows, :], across, preferred_element_type=F32
            )
            product -= x_slots[slot, half, :, cols].astype(F32) * shift
            out[:, cols] = product.astype(out.dtype)


def backward_tick(tick, ids, grad, stash, weights, deltas):
    first = not deltas
    return pl.pallas_call(
        functools.partial(backward_kernel, tick, first),
        out_shape=(
            jax.ShapeDtypeStruct((MB, HALF), F32),
            jax.ShapeDtypeStruct((MB, HALF), BF16),
            jax.ShapeDtypeStruct((MICRO + 1, MB, HALF), BF16),
        ),
        in_specs=[SMEM] + [VMEM] * (6 + len(deltas)),
        out_specs=(VMEM,) * 3,
        scratch_shapes=[pltpu.VMEM((MB, HALF), BF16)],
        input_output_aliases={} if first else {7: 2},
        compiler_params=PARAMS,
        cost_estimate=pl.CostEstimate(
            flops=2 * MB * D * HALF, bytes_accessed=2 * D * HALF, transcendentals=MB * HALF
        ),
        name="backward_tick",
    )(ids, grad, *stash, *weights, *deltas)


def swap_cores(value):
    return lax.ppermute(value, "tp", [(0, 1), (1, 0)])


def to_section(value, step):
    return lax.ppermute(value, "section", [(s, (s + step) % SECTIONS) for s in range(SECTIONS)])


def along_y(value, step):
    pairs = [(i, (i // SIDE + step) % SIDE * SIDE + i % SIDE) for i in range(ISLANDS)]
    return lax.ppermute(value, "island", pairs)


def along_z(value, step):
    pairs = [(i, i // SIDE * SIDE + (i % SIDE + step) % SIDE) for i in range(ISLANDS)]
    return lax.ppermute(value, "island", pairs)


def ring_gather(block, shift, place, target, at):
    half = block.shape[0] // 2
    below, above = shift(block, 1), shift(block, -1)
    far_low, far_high = shift(below[:half], 1), shift(above[half:], -1)
    target = at(target, place, block, 0)
    target = at(target, (place + SIDE - 1) % SIDE, below, 0)
    target = at(target, (place + 1) % SIDE, above, 0)
    target = at(target, (place + 2) % SIDE, far_low, 0)
    return at(target, (place + 2) % SIDE, far_high, half)


def gather_islands(block, target, row_start):
    island = lax.axis_index("island")
    y_place, z_place = island // SIDE, island % SIDE
    tail = (1,) * (target.ndim - 4)

    def at_z(buffer, position, piece, start):
        return lax.dynamic_update_slice(buffer, piece[None], (position, start, 0))

    def at_y(buffer, position, piece, start):
        piece = piece.reshape(1, *piece.shape[:1], *tail, *piece.shape[1:])
        return lax.dynamic_update_slice(
            buffer, piece, (position, start, row_start) + (0,) * (buffer.ndim - 3)
        )

    column = ring_gather(block, along_z, z_place, jnp.zeros((SIDE, *block.shape), BF16), at_z)
    return ring_gather(column, along_y, y_place, target, at_y), column


def after(value, earlier):
    return lax.optimization_barrier((value, earlier))[0]


def gather_weights(rows):
    by_gather = lax.all_gather(rows[:, :SPLIT], "island", axis=0, tiled=True)
    by_rings = jnp.zeros((SIDE, SIDE, ROWS, HALF - SPLIT), BF16)
    start = 0
    for size in ROW_CHUNKS:
        block = rows[start : start + size, SPLIT:]
        by_rings, _ = gather_islands(block, by_rings, start)
        start += size
    return by_gather, by_rings.reshape(D, HALF - SPLIT)


def exchange_x(x_slots, tp_id, earlier):
    count = MICRO // 2
    part = lax.dynamic_slice_in_dim(x_slots, tp_id * count, count, 0)
    part = part.reshape(count, 2, MB, ISLANDS // 2, ROWS).transpose(1, 3, 0, 2, 4)
    part = after(part.reshape(ISLANDS, count * MB, ROWS), earlier)
    return lax.all_to_all(part, "island", 0, 0)


def body(tokens, cotangent, master):
    island_count = lax.axis_size("island")
    section_id = lax.axis_index("section")
    tp_id = lax.axis_index("tp")
    ids = jnp.stack([tp_id, section_id]).astype(jnp.int32)
    tok_blocks = [tokens[m * MB : (m + 1) * MB] for m in range(MICRO)]
    cot_blocks = [cotangent[m * MB : (m + 1) * MB] for m in range(MICRO)]
    weights = gather_weights(master[0].astype(BF16))

    tok_blocks, cot_blocks = lax.optimization_barrier((tok_blocks, cot_blocks))
    stash, deltas = (), None
    grads = jnp.zeros((MICRO + 1, MB, HALF), BF16)
    own, grad = tok_blocks[0], cot_blocks[0]
    for tick in range(TICKS):
        if tick < FORWARD_TICKS:
            other = swap_cores(own)
            following = tok_blocks[min(tick + 1, MICRO - 1)]
            send, *stash = forward_tick(tick, ids, own, other, following, weights, stash)
            if tick < FORWARD_TICKS - 1:
                own = to_section(send, 1)
        if tick >= SECTIONS:
            own_part, other_part, deltas = backward_tick(
                tick, ids, grad, stash, weights, () if deltas is None else (deltas,)
            )
            received = swap_cores(other_part)
            grad_out = (grad.astype(F32) + own_part + received.astype(F32)).astype(BF16)
            slot = slot_of(backward_micro(tick, section_id))
            grads = lax.dynamic_update_slice_in_dim(grads, grad_out[None], slot, 0)
            if tick < TICKS - 1:
                following = cot_blocks[min(tick + 1 - SECTIONS, MICRO - 1)]
                passed = jnp.where(section_id == 0, following, grad_out)
                grad = to_section(passed, -1)
        micro = tick - (2 * SECTIONS - 1)
        if micro == EARLY - 1:
            early_deltas = lax.all_gather(deltas[:EARLY], "island")

    x_slots, deltas, empty = lax.optimization_barrier((stash[0], deltas, jnp.zeros((), BF16)))
    ring_deltas = jnp.broadcast_to(empty, (SIDE, SIDE, MICRO - EARLY, MB, HALF))
    block = deltas[EARLY]
    for micro in range(EARLY, MICRO):
        ring_deltas, column = gather_islands(block, ring_deltas, micro - EARLY)
        if micro < MICRO - 1:
            block = after(deltas[micro + 1], column)
    x_part = exchange_x(x_slots, tp_id, column)

    x_other = swap_cores(x_part)

    def outer(x_rows, delta_rows):
        return lax.dot_general(
            x_rows.reshape(-1, ROWS),
            delta_rows.reshape(-1, HALF),
            (((0,), (0,)), ((), ())),
            preferred_element_type=F32,
        )

    late_rows = outer(jnp.where(tp_id == 1, x_part, x_other), ring_deltas)
    late_rows = lax.optimization_barrier(late_rows)
    grad_rows = late_rows + outer(jnp.where(tp_id == 0, x_part, x_other), early_deltas)
    updated = master[0] - STEP_SIZE * grad_rows / (MICRO * MB * island_count)
    return (grads[:MICRO].reshape(1, MICRO * MB, HALF), updated[None])


def solution(mesh):
    placed = (P("island", "tp"), P("island", "tp"), P("section", "island", "tp"))
    return jax.shard_map(
        body,
        mesh=mesh,
        in_specs=placed,
        out_specs=(P("section", "island", "tp"), P("section", "island", "tp")),
        check_vma=False,
    )
```

```python
import functools

import jax
import jax.numpy as jnp
from jax import lax
from jax.experimental import pallas as pl
from jax.experimental.pallas import tpu as pltpu
from jax.sharding import PartitionSpec as P

D = 3584
HALF = 1792
MICRO = 4
MB = 48
SECTIONS = 8
ISLANDS = 16
SIDE = 4
ROWS = D // ISLANDS
FORWARD_TICKS = MICRO + SECTIONS - 1
TICKS = FORWARD_TICKS + SECTIONS
SPLIT = 1024
ROW_CHUNKS = (96, 128)
EARLY = 2
NORM_EPS = 1e-05
STEP_SIZE = 1.0
F32 = jnp.float32
BF16 = jnp.bfloat16
N_TILE = 256
K_TILE = 256
LIMIT_MB = 8
PARAMS = pltpu.CompilerParams(vmem_limit_bytes=LIMIT_MB * 1024 * 1024)
VMEM = pl.BlockSpec(memory_space=pltpu.VMEM)
SMEM = pl.BlockSpec(memory_space=pltpu.SMEM)


def half_rows(half, start, size):
    return pl.ds(pl.multiple_of(half * HALF + start, 256), size)


def slot_of(micro):
    return jnp.where((micro >= 0) & (micro < MICRO), micro, MICRO)


def backward_micro(tick, section):
    return tick - (2 * SECTIONS - 1) + section


def forward_kernel(
    tick, first, ids, own, other, next_tokens, weights_a, weights_b, *refs
):
    send, x_slots, preacts, scales = refs if first else refs[3:]
    tp_id = ids[0]
    is_last = ids[1] == SECTIONS - 1
    slot = slot_of(tick - ids[1])
    x_slots[slot, tp_id] = own[...]
    x_slots[slot, 1 - tp_id] = other[...]
    own_float = own[...].astype(F32)
    other_float = other[...].astype(F32)
    square_sum = jnp.sum(own_float * own_float, axis=1, keepdims=True)
    square_sum += jnp.sum(other_float * other_float, axis=1, keepdims=True)
    row_scale = lax.rsqrt(square_sum / D + NORM_EPS)
    scales[slot] = jnp.broadcast_to(row_scale, scales.shape[1:])
    for start in range(0, HALF, N_TILE):
        cols = pl.ds(start, N_TILE)
        weights = weights_a if start < SPLIT else weights_b
        part = pl.ds(start if start < SPLIT else start - SPLIT, N_TILE)
        product = jnp.dot(
            own[...], weights[half_rows(tp_id, 0, HALF), part], preferred_element_type=F32
        )
        product += jnp.dot(
            other[...], weights[half_rows(1 - tp_id, 0, HALF), part], preferred_element_type=F32
        )
        value = product * row_scale
        preacts[slot, :, cols] = value
        output = own[:, cols].astype(F32) + value / (1.0 + jnp.exp(-value))
        output = output.astype(BF16).astype(F32)
        send[:, cols] = jnp.where(is_last, next_tokens[:, cols].astype(F32), output).astype(BF16)


STASH = (
    jax.ShapeDtypeStruct((MICRO + 1, 2, MB, HALF), BF16),
    jax.ShapeDtypeStruct((MICRO + 1, MB, HALF), F32),
    jax.ShapeDtypeStruct((MICRO + 1, MB, 128), F32),
)


def forward_tick(tick, ids, own, other, next_tokens, weights, stash):
    first = not stash
    return pl.pallas_call(
        functools.partial(forward_kernel, tick, first),
        out_shape=(jax.ShapeDtypeStruct(own.shape, BF16), *STASH),
        in_specs=[SMEM] + [VMEM] * (5 + len(stash)),
        out_specs=(VMEM,) * 4,
        input_output_aliases={} if first else {6: 1, 7: 2, 8: 3},
        compiler_params=PARAMS,
        cost_estimate=pl.CostEstimate(
            flops=2 * MB * D * HALF, bytes_accessed=2 * D * HALF, transcendentals=MB * HALF
        ),
        name="forward_tick",
    )(ids, own, other, next_tokens, *weights, *stash)


def backward_kernel(
    tick, first, ids, grad, x_slots, preacts, scales, weights_a, weights_b, *refs
):
    own_part, other_part, deltas, scaled = refs if first else refs[1:]
    tp_id = ids[0]
    slot = slot_of(backward_micro(tick, ids[1]))
    row_scale = scales[slot, :, :1]
    mean_prod = jnp.zeros((MB, 1), F32)
    for start in range(0, HALF, N_TILE):
        cols = pl.ds(start, N_TILE)
        value = preacts[slot, :, cols]
        sig_value = 1.0 / (1.0 + jnp.exp(-value))
        delta = grad[:, cols].astype(F32) * (sig_value * (1.0 + value * (1.0 - sig_value)))
        mean_prod += jnp.sum(delta * value, axis=1, keepdims=True)
        scaled[:, cols] = (delta * row_scale).astype(BF16)
    shift = row_scale * row_scale * (mean_prod / D)
    deltas[slot] = scaled[...]
    across = (((1,), (1,)), ((), ()))
    for start in range(0, HALF, K_TILE):
        cols = pl.ds(start, K_TILE)
        for half, out in ((1 - tp_id, other_part), (tp_id, own_part)):
            rows = half_rows(half, start, K_TILE)
            product = lax.dot_general(
                scaled[:, :SPLIT], weights_a[rows, :], across, preferred_element_type=F32
            )
            product += lax.dot_general(
                scaled[:, SPLIT:], weights_b[rows, :], across, preferred_element_type=F32
            )
            product -= x_slots[slot, half, :, cols].astype(F32) * shift
            out[:, cols] = product.astype(out.dtype)


def backward_tick(tick, ids, grad, stash, weights, deltas):
    first = not deltas
    return pl.pallas_call(
        functools.partial(backward_kernel, tick, first),
        out_shape=(
            jax.ShapeDtypeStruct((MB, HALF), F32),
            jax.ShapeDtypeStruct((MB, HALF), BF16),
            jax.ShapeDtypeStruct((MICRO + 1, MB, HALF), BF16),
        ),
        in_specs=[SMEM] + [VMEM] * (6 + len(deltas)),
        out_specs=(VMEM,) * 3,
        scratch_shapes=[pltpu.VMEM((MB, HALF), BF16)],
        input_output_aliases={} if first else {7: 2},
        compiler_params=PARAMS,
        cost_estimate=pl.CostEstimate(
            flops=2 * MB * D * HALF, bytes_accessed=2 * D * HALF, transcendentals=MB * HALF
        ),
        name="backward_tick",
    )(ids, grad, *stash, *weights, *deltas)


def swap_cores(value):
    return lax.ppermute(value, "tp", [(0, 1), (1, 0)])


def to_section(value, step):
    return lax.ppermute(value, "section", [(s, (s + step) % SECTIONS) for s in range(SECTIONS)])


def along_y(value, step):
    pairs = [(i, (i // SIDE + step) % SIDE * SIDE + i % SIDE) for i in range(ISLANDS)]
    return lax.ppermute(value, "island", pairs)


def along_z(value, step):
    pairs = [(i, i // SIDE * SIDE + (i % SIDE + step) % SIDE) for i in range(ISLANDS)]
    return lax.ppermute(value, "island", pairs)


def ring_gather(block, shift, place, target, at):
    half = block.shape[0] // 2
    below, above = shift(block, 1), shift(block, -1)
    far_low, far_high = shift(below[:half], 1), shift(above[half:], -1)
    target = at(target, place, block, 0)
    target = at(target, (place + SIDE - 1) % SIDE, below, 0)
    target = at(target, (place + 1) % SIDE, above, 0)
    target = at(target, (place + 2) % SIDE, far_low, 0)
    return at(target, (place + 2) % SIDE, far_high, half), (below, above)


def gather_islands(block, target, row_start):
    island = lax.axis_index("island")
    y_place, z_place = island // SIDE, island % SIDE
    tail = (1,) * (target.ndim - 4)

    def at_z(buffer, position, piece, start):
        return lax.dynamic_update_slice(buffer, piece[None], (position, start, 0))

    def at_y(buffer, position, piece, start):
        piece = piece.reshape(1, *piece.shape[:1], *tail, *piece.shape[1:])
        return lax.dynamic_update_slice(
            buffer, piece, (position, start, row_start) + (0,) * (buffer.ndim - 3)
        )

    start = jnp.zeros((SIDE, *block.shape), BF16)
    column, first_round = ring_gather(block, along_z, z_place, start, at_z)
    return ring_gather(column, along_y, y_place, target, at_y)[0], column, first_round


def after(value, earlier):
    return lax.optimization_barrier((value, earlier))[0]


def gather_weights(rows):
    by_gather = lax.all_gather(rows[:, :SPLIT], "island", axis=0, tiled=True)
    by_rings = jnp.zeros((SIDE, SIDE, ROWS, HALF - SPLIT), BF16)
    start = 0
    for size in ROW_CHUNKS:
        block = rows[start : start + size, SPLIT:]
        by_rings, _, _ = gather_islands(block, by_rings, start)
        start += size
    return by_gather, by_rings.reshape(D, HALF - SPLIT)


def exchange_x(x_slots, tp_id, earlier):
    count = MICRO // 2
    part = lax.dynamic_slice_in_dim(x_slots, tp_id * count, count, 0)
    part = part.reshape(count, 2, MB, ISLANDS // 2, ROWS).transpose(1, 3, 0, 2, 4)
    part = after(part.reshape(ISLANDS, count * MB, ROWS), earlier)
    return lax.all_to_all(part, "island", 0, 0)


def body(tokens, cotangent, master):
    island_count = lax.axis_size("island")
    section_id = lax.axis_index("section")
    tp_id = lax.axis_index("tp")
    ids = jnp.stack([tp_id, section_id]).astype(jnp.int32)
    tok_blocks = [tokens[m * MB : (m + 1) * MB] for m in range(MICRO)]
    cot_blocks = [cotangent[m * MB : (m + 1) * MB] for m in range(MICRO)]
    weights = gather_weights(master[0].astype(BF16))

    tok_blocks, cot_blocks = lax.optimization_barrier((tok_blocks, cot_blocks))
    stash, deltas = (), None
    grads = jnp.zeros((MICRO + 1, MB, HALF), BF16)
    own, grad = tok_blocks[0], cot_blocks[0]
    for tick in range(TICKS):
        if tick < FORWARD_TICKS:
            other = swap_cores(own)
            following = tok_blocks[min(tick + 1, MICRO - 1)]
            send, *stash = forward_tick(tick, ids, own, other, following, weights, stash)
            if tick < FORWARD_TICKS - 1:
                own = to_section(send, 1)
        if tick >= SECTIONS:
            own_part, other_part, deltas = backward_tick(
                tick, ids, grad, stash, weights, () if deltas is None else (deltas,)
            )
            received = swap_cores(other_part)
            grad_out = (grad.astype(F32) + own_part + received.astype(F32)).astype(BF16)
            slot = slot_of(backward_micro(tick, section_id))
            grads = lax.dynamic_update_slice_in_dim(grads, grad_out[None], slot, 0)
            if tick < TICKS - 1:
                following = cot_blocks[min(tick + 1 - SECTIONS, MICRO - 1)]
                passed = jnp.where(section_id == 0, following, grad_out)
                grad = to_section(passed, -1)
        micro = tick - (2 * SECTIONS - 1)
        if micro == EARLY - 1:
            early_deltas = lax.all_gather(deltas[:EARLY], "island")

    x_slots, deltas, empty = lax.optimization_barrier((stash[0], deltas, jnp.zeros((), BF16)))
    ring_deltas = jnp.broadcast_to(empty, (SIDE, SIDE, MICRO - EARLY, MB, HALF))
    block = deltas[EARLY]
    for micro in range(EARLY, MICRO):
        ring_deltas, column, first_round = gather_islands(block, ring_deltas, micro - EARLY)
        if micro < MICRO - 1:
            block = after(deltas[micro + 1], first_round)
    x_part = exchange_x(x_slots, tp_id, column)

    x_other = swap_cores(x_part)

    def outer(x_rows, delta_rows):
        return lax.dot_general(
            x_rows.reshape(-1, ROWS),
            delta_rows.reshape(-1, HALF),
            (((0,), (0,)), ((), ())),
            preferred_element_type=F32,
        )

    late_rows = outer(jnp.where(tp_id == 1, x_part, x_other), ring_deltas)
    late_rows = lax.optimization_barrier(late_rows)
    grad_rows = late_rows + outer(jnp.where(tp_id == 0, x_part, x_other), early_deltas)
    updated = master[0] - STEP_SIZE * grad_rows / (MICRO * MB * island_count)
    return (grads[:MICRO].reshape(1, MICRO * MB, HALF), updated[None])


def solution(mesh):
    placed = (P("island", "tp"), P("island", "tp"), P("section", "island", "tp"))
    return jax.shard_map(
        body,
        mesh=mesh,
        in_specs=placed,
        out_specs=(P("section", "island", "tp"), P("section", "island", "tp")),
        check_vma=False,
    )
```
